256 devices in a mesh: wide: 64 (over z, y, x_hi), narrow: 4 (over x_lo, core).
Axes of the slice: x: 4 (x_hi: 2, x_lo: 2; x = x_hi * 2 + x_lo), y: 4, z: 8, core: 2. Of those that a mesh axis runs over, the one named last changes fastest.
Arguments:
- embeddings: bfloat16 [32768, 4096], P(('wide', 'narrow')), may hold values from -6 to 6
- projection: bfloat16 [4096, 1024], P('wide'), as said below
- centroids: bfloat16 [8192, 1024], P('narrow'), as said below
- target: bfloat16 [32768, 8192], P('wide', 'narrow'), as said below
Outputs:
- grad_projected: float32 [32768, 1024], P(('wide', 'narrow'))
- grad_centroids: float32 [8192, 1024], P('narrow', 'wide')
- loss: float32 [], replicated
The draws below stay inside these ranges and needn't reach their ends.
Inputs may be any that keep to these rules, and one draw needn't show every extreme that they name: Weights of each centroid row and projection are of the scale 1 / sqrt(1024) and 1 / sqrt(4194304). `target`: every entry is positive. `centroids`: finite values.
All inputs are finite; a program needn't handle non-finite values.
Results may differ from the reference program's by a relative error of at most 0.0065.
Values may be sent and summed in bfloat16 or wider, within the bound.
A program may use at most 64 MiB of HBM per device.

```python
import math
import jax
import jax.numpy as jnp
from jax import lax

DIN = 4096
DZ = 1024
K = 8192
TOK_DEV = 128
DOCS = 32768


def draw_projection(key, part):
    key = jax.random.fold_in(key, 11)
    factor = 1.0 / jnp.sqrt(jnp.float32(DIN * DZ))
    values = jax.random.truncated_normal(key, -6.0, 6.0, (DIN, DZ), jnp.float32)
    return (values * factor).astype(jnp.bfloat16)


def draw_centroids(key, part):
    key = jax.random.fold_in(key, 23)
    first = jax.random.fold_in(key, 0)
    factor = 1.0 / jnp.sqrt(jnp.float32(DZ))
    values = jax.random.truncated_normal(first, -6.0, 6.0, (K, DZ), jnp.float32)
    return (values * factor).astype(jnp.bfloat16)


def row_sharpness(key, growth):
    ramp = jnp.arange(DOCS, dtype=jnp.float32) / jnp.float32(DOCS)
    blocks = jax.random.uniform(key, (DOCS // TOK_DEV,), jnp.float32, -0.3, 0.3)
    jitter = jnp.repeat(blocks, TOK_DEV)
    return jnp.exp(ramp * math.log(growth) + jitter)


def draw_target(key, part):
    key = jax.random.fold_in(key, 37)
    first, second = jax.random.split(key)
    sharp = row_sharpness(second, 3.2)
    values = jax.random.truncated_normal(first, -6.0, 6.0, (DOCS, K), jnp.float32)
    return jnp.exp(sharp[:, None] * values).astype(jnp.bfloat16)


def block_levels(key, shape, cuts, least, top_value):
    gain, own = 1.0, jax.random.fold_in(key, 6)
    for position, shards_of in cuts:
        heights = jnp.exp(jax.random.uniform(jax.random.fold_in(own, position), (shards_of,), jnp.float32, least / len(cuts), top_value / len(cuts)))
        gain = gain * jnp.repeat(heights, shape[position] // shards_of).reshape([-1 if axis == position else 1 for axis in range(len(shape))])
    return gain


def normal_values(own_key, extent, width, limit, cuts=(), kind=jnp.bfloat16):
    result = width * jax.random.normal(own_key, extent, jnp.float32)
    if cuts:
        result = result * block_levels(own_key, extent, cuts, -0.22, 0.18)
    return jnp.clip(result, -limit, limit).astype(kind)


def setup_inputs(seed: int = 0) -> dict:
    key_list = jax.random.split(jax.random.key(seed), 5)
    embeddings = normal_values(key_list[0], (DOCS, DIN), 1.0, 6.0, ((0, 256),))
    projection = draw_projection(jax.random.fold_in(key_list[4], 71), 0)
    centroids = draw_centroids(jax.random.fold_in(key_list[4], 71), 0)
    target = draw_target(jax.random.fold_in(key_list[4], 71), 0)
    return dict(embeddings=embeddings, projection=projection, centroids=centroids, target=target)


loss_scale = 64.0


def reference(embeddings, projection, centroids, target):
    total = embeddings.shape[0]
    block = math.gcd(total, 1024)
    count = total // block
    cent_f = centroids.astype(jnp.float32)
    cnorm = jnp.sum(cent_f * cent_f, axis=1)

    def step(carry, index):
        accum, colsum, lsum = carry
        start = (index * block).astype(jnp.int32)
        emb = lax.dynamic_slice_in_dim(embeddings, start, block, 0)
        tgt = lax.dynamic_slice_in_dim(target, start, block, 0)
        feats = jnp.dot(emb, projection, preferred_element_type=jnp.float32).astype(jnp.bfloat16)
        feat_f = feats.astype(jnp.float32)
        znorm = jnp.sum(feat_f * feat_f, axis=1)
        inner = jnp.dot(feats, centroids.T, preferred_element_type=jnp.float32)
        dist = znorm[:, None] + cnorm[None, :] - 2.0 * inner
        kernel = 1.0 / (1.0 + dist)
        weights = tgt.astype(jnp.float32)
        wsum = jnp.sum(weights, axis=1)
        ksum = jnp.sum(kernel, axis=1)
        cross = jnp.sum(weights * (jnp.log(weights) + jnp.log(1.0 + dist)), axis=1)
        row_loss = cross / wsum - jnp.log(wsum) + jnp.log(ksum)
        coeff = (loss_scale * kernel * (weights / wsum[:, None] - kernel / ksum[:, None])).astype(jnp.bfloat16)
        coeff_f = coeff.astype(jnp.float32)
        rowg = jnp.sum(coeff_f, axis=1)
        pull = jnp.dot(coeff, centroids, preferred_element_type=jnp.float32)
        grad_rows = 2.0 * (rowg[:, None] * feat_f - pull)
        accum = accum + jnp.dot(coeff.T, feats, preferred_element_type=jnp.float32)
        colsum = colsum + jnp.sum(coeff_f, axis=0)
        return (accum, colsum, lsum + jnp.sum(row_loss)), grad_rows

    init = (jnp.zeros(centroids.shape, jnp.float32), jnp.zeros((centroids.shape[0],), jnp.float32), jnp.zeros((), jnp.float32))
    (accum, colsum, lsum), grads = lax.scan(step, init, jnp.arange(count, dtype=jnp.int32))
    grad_projected = grads.reshape(total, centroids.shape[1])
    grad_centroids = -2.0 * (accum - colsum[:, None] * cent_f)
    return grad_projected, grad_centroids, lsum / total
```

```python
import jax
import jax.numpy as jnp
from jax import lax
from jax.experimental import pallas as pl
from jax.experimental.pallas import tpu as pltpu
from jax.sharding import PartitionSpec as P

NZ, NY, NX = 8, 4, 4
DIN, DZ, HALF = 4096, 1024, 512
DOCS_DEV, CHIP_DOCS, RING_DOCS = 128, 256, 1024
CENTS = 1024
DOCS = 32768
SCALE = 64.0
ROWS_B = 48
ROWS_A = 80
A_PLUS = 48
ORDER = (4, 3, -3, 2, -2, 1, -1, 0)
N_SEM = 160
bf16, f32 = jnp.bfloat16, jnp.float32


def body(
    emb, proj, cent, target,
    gp_ref, gc_ref, loss_ref,
    pbuf, ebuf, cbuf, ct, tbuf, feat, ft, kbuf, cbf, stats, ab, rowg_ref, cn_ref, colg_ref,
    rs, rfwd, rone, rcomb, csend, zsend, zrecv, ysum, xsend, xrecv,
    psend, pown, precv, gsend, gx, ly, lz,
    send_sems, recv_sems, local_sems,
):
    wide, narrow = lax.axis_index("wide"), lax.axis_index("narrow")
    z, y, xh = wide // 8, (wide // 2) % 4, wide % 2
    xl, core = narrow // 2, narrow % 2
    x = xh * 2 + xl

    def device(dx=0, dy=0, dz=0, dc=0):
        tx, ty, tz, tc = (x + dx + NX) % NX, (y + dy + NY) % NY, (z + dz + NZ) % NZ, (core + dc) % 2
        return (tz * 8 + ty * 2 + tx // 2, (tx % 2) * 2 + tc)

    def to_device(tx):
        return (z * 8 + y * 2 + tx // 2, (tx % 2) * 2 + core)

    def zi(dz):
        return (z + dz + NZ) % NZ

    def yi(dy):
        return (y + dy + NY) % NY

    def xi(dx):
        return (x + dx + NX) % NX

    copies = []

    def send(src, dst, target_device):
        number = len(copies)
        copy = pltpu.make_async_remote_copy(
            src_ref=src, dst_ref=dst, send_sem=send_sems.at[number], recv_sem=recv_sems.at[number],
            device_id=target_device, device_id_type=pl.DeviceIdType.MESH,
        )
        copy.start()
        copies.append(copy)
        return copy

    locals_ = []

    def local(src, dst):
        copy = pltpu.make_async_copy(src, dst, local_sems.at[len(locals_)])
        copy.start()
        locals_.append(copy)
        return copy

    own_rows = pl.ds(pl.multiple_of(xh * 64, 64), 64)
    own_cols = pl.ds(pl.multiple_of(core * HALF, HALF), HALF)
    l_proj = local(proj.at[:, own_cols], pbuf.at[z, y, own_rows])
    l_emb = local(emb, ebuf.at[pl.ds(pl.multiple_of(core * 128, 128), 128)])
    j_rows = pl.ds(pl.multiple_of(xh * CENTS, CENTS), CENTS)
    other_rows = pl.ds(pl.multiple_of((1 - xh) * CENTS, CENTS), CENTS)
    my_docs = pl.ds(pl.multiple_of(xh * 512, 512), 512)
    l_cent = local(cent.at[j_rows], cbuf)
    l_tgt = local(target.at[:, j_rows], tbuf.at[my_docs])

    ring = [(dx, dc) for dx in range(NX) for dc in range(2) if (dx, dc) != (0, 0)]
    peers = [device(dx=dx, dc=dc) for dx, dc in ring]
    peers += [device(dz=d) for d in range(1, NZ)] + [device(dy=d) for d in range(1, NY)]
    barrier = pltpu.get_barrier_semaphore()
    for peer in peers:
        pl.semaphore_signal(barrier, inc=1, device_id=peer, device_id_type=pl.DeviceIdType.MESH)
    pl.semaphore_wait(barrier, len(peers))

    a_start = pl.multiple_of((1 - xh) * 48, 16)
    b_start = pl.multiple_of(xh * 80, 16)

    def rows_of(part):
        if part == "a":
            return pl.ds(a_start, ROWS_A)
        if part == "a+":
            return pl.ds(a_start, A_PLUS)
        if part == "a-":
            return pl.ds(pl.multiple_of(a_start + A_PLUS, 16), ROWS_A - A_PLUS)
        return pl.ds(b_start, ROWS_B)

    def move(part, at_z, at_y, **hop):
        where = pbuf.at[zi(at_z), yi(at_y), rows_of(part)]
        return send(where, where, device(**hop))

    bz, az, ay, by = {}, {}, {}, {}

    def b_start_chain(q):
        bz[q, 1, 1] = move("b", 0, q, dz=1)
        bz[q, -1, 1] = move("b", 0, q, dz=-1)

    l_proj.wait()
    where = pbuf.at[z, y, own_rows]
    b_start_chain(0)
    for hop in (1, -1, 2):
        by[hop] = move("b", 0, 0, dy=hop)
    x_swap = send(where, where, to_device(3 - x))
    l_emb.wait()
    mine = ebuf.at[pl.ds(pl.multiple_of(core * 128, 128), 128)]
    e_copy = send(mine, mine, device(dc=1))
    l_tgt.wait()
    t_copy = send(target.at[:, other_rows], tbuf.at[my_docs], device(dx=2))

    x_swap.wait_recv()

    def a_y_sends(dz):
        ay[dz, 1] = move("a", dz, 0, dy=1)
        ay[dz, -1] = move("a", dz, 0, dy=-1)

    def a_y_forward(dz):
        if dz % 2 == 0:
            ay[dz, 1].wait_recv()
            ay[dz, 2] = move("a", dz, -1, dy=1)
        else:
            ay[dz, -1].wait_recv()
            ay[dz, 2] = move("a", dz, 1, dy=-1)

    az[1, 1] = move("a", 0, 0, dz=1)
    az[-1, 1] = move("a", 0, 0, dz=-1)
    a_y_sends(0)
    by[1].wait_recv()
    b_start_chain(-1)
    by[-1].wait_recv()
    b_start_chain(1)
    by[2].wait_recv()
    b_start_chain(2)

    def b_step(step, q):
        for sign in (1, -1):
            if (q, sign, step) in bz:
                bz[q, sign, step].wait_recv()
                if step < 3 or (step == 3 and (sign == 1) == (q in (0, 2))):
                    bz[q, sign, step + 1] = move("b", -sign * step, q, dz=sign)

    def a_step(step):
        for sign in (1, -1):
            az[sign, step].wait_recv()
            if step < 3:
                az[sign, step + 1] = move("a", -sign * step, 0, dz=sign)
            elif step == 3:
                az[sign, 4] = move("a+" if sign == 1 else "a-", -sign * step, 0, dz=sign)
        if step < 4:
            a_y_sends(step)
            a_y_sends(-step)
        else:
            a_y_sends(4)

    def target_stats(block):
        rows = pl.ds(pl.multiple_of(block * 128, 128), 128)
        wp = jnp.zeros((128, 128), f32)
        lp = jnp.zeros((128, 128), f32)
        for lane in range(8):
            t = tbuf[rows, lane * 128:(lane + 1) * 128].astype(f32)
            wp = wp + t
            lp = lp + t * jnp.log(t)
        stats[me8, 0:1, rows] = jnp.sum(wp.T, axis=0, keepdims=True)
        stats[me8, 1:2, rows] = jnp.sum(lp.T, axis=0, keepdims=True)

    me8 = x * 2 + core
    stats[me8] = jnp.zeros((8, RING_DOCS), f32)

    def centroid_block(j):
        cols = pl.ds(pl.multiple_of(j * 128, 128), 128)
        c = cbuf[cols, :].astype(f32).T
        ct[:, cols] = c.astype(bf16)
        cn_ref[0:1, cols] = jnp.sum(c * c, axis=0, keepdims=True)

    l_cent.wait()
    for step in (1, 2, 3, 4):
        b_step(step, 0)
        a_step(step)
        for q in (-1, 1, 2):
            b_step(step, q)
        if step == 1:
            a_y_forward(0)
        else:
            a_y_forward(step - 1)
            a_y_forward(-(step - 1))
        centroid_block(2 * step - 2)
        centroid_block(2 * step - 1)
        target_stats(xh * 4 + step - 1)
    a_y_forward(4)
    t_copy.wait_recv()

    @pl.loop(0, 4)
    def _(i):
        target_stats((1 - xh) * 4 + i)

    e_copy.wait_recv()
    for dz in (0, 1, -1, 2, -2, 3, -3, 4):
        ay[dz, -1 if dz % 2 == 0 else 1].wait_recv()
        ay[dz, 2].wait_recv()

    def chip_rows(dx):
        return pl.ds(pl.multiple_of(xi(dx) * CHIP_DOCS, CHIP_DOCS), CHIP_DOCS)

    own = jnp.dot(ebuf[...], pbuf[...].reshape(DIN, HALF), preferred_element_type=f32).astype(bf16)
    feat[core, chip_rows(0), :] = own
    fx = {}

    def feat_send(at_x, **hop):
        where = feat.at[core, chip_rows(at_x)]
        return send(where, where, device(**hop))

    fx[1] = feat_send(0, dx=1)
    fx[3] = feat_send(0, dx=-1)
    fc = {0: feat_send(0, dc=1)}
    fx[2] = feat_send(0, dx=2)

    def inner(dx):
        fc[dx].wait_recv()
        rows = chip_rows(dx)
        f0, f1 = feat[0, rows, :], feat[1, rows, :]
        g = jnp.dot(f0, ct[0:HALF, :], preferred_element_type=f32)
        g = g + jnp.dot(f1, ct[HALF:DZ, :], preferred_element_type=f32)
        g0, g1 = f0.astype(f32), f1.astype(f32)
        zn = 1.0 + jnp.sum(g0 * g0 + g1 * g1, axis=1, keepdims=True)
        kp = jnp.zeros((CHIP_DOCS, 128), f32)
        cp = jnp.zeros((CHIP_DOCS, 128), f32)
        for lane in range(8):
            cols = slice(lane * 128, (lane + 1) * 128)
            u = (zn + cn_ref[0:1, cols]) - 2.0 * g[:, cols]
            r = pl.reciprocal(u, approx=True)
            k = r * (2.0 - u * r)
            kbuf[rows, cols] = k
            kp = kp + k
            cp = cp + tbuf[rows, cols].astype(f32) * jnp.log(u)
        stats[me8, 2:3, rows] = jnp.sum(kp.T, axis=0, keepdims=True)
        stats[me8, 3:4, rows] = jnp.sum(cp.T, axis=0, keepdims=True)

    def transpose_features(dx):
        rows = chip_rows(dx)
        ft[0:HALF, rows] = feat[0, rows, :].astype(f32).T.astype(bf16)
        ft[HALF:DZ, rows] = feat[1, rows, :].astype(f32).T.astype(bf16)

    inner(0)
    transpose_features(0)
    for dx in (1, 3, 2):
        fx[dx].wait_recv()
        fc[NX - dx] = feat_send(NX - dx, dc=1)
        inner(NX - dx)
        if dx != 2:
            transpose_features(NX - dx)

    st = []
    for dx, dc in ring:
        st.append(send(stats.at[me8], stats.at[me8], device(dx=dx, dc=dc)))
    transpose_features(2)
    for copy in st:
        copy.wait_recv()
    tot = stats[0]
    for i in range(1, 8):
        tot = tot + stats[i]
    wsum, tlog, ksum, clog = tot[0:1], tot[1:2], tot[2:3], tot[3:4]
    row_loss = (tlog + clog) / wsum - jnp.log(wsum) + jnp.log(ksum)
    ly[y] = jnp.broadcast_to(jnp.sum(row_loss, axis=1, keepdims=True), (8, 128))
    lsy = [send(ly.at[y], ly.at[y], device(dy=d)) for d in range(1, NY)]
    ra, rb = SCALE / wsum, SCALE / ksum
    for block in range(8):
        rows = slice(block * 128, (block + 1) * 128)
        ab[0, rows, :] = jnp.broadcast_to(ra[:, rows], (128, 128)).T
        ab[1, rows, :] = jnp.broadcast_to(rb[:, rows], (128, 128)).T

    colg_ref[...] = jnp.zeros((8, CENTS), f32)

    @pl.loop(0, 8)
    def _(block):
        rows = pl.ds(pl.multiple_of(block * 128, 128), 128)
        a, b = ab[0, rows, :], ab[1, rows, :]
        rp = jnp.zeros((128, 128), f32)
        for lane in range(8):
            cols = slice(lane * 128, (lane + 1) * 128)
            k = kbuf[rows, cols]
            cf = (k * (tbuf[rows, cols].astype(f32) * a - k * b)).astype(bf16)
            cbf[rows, cols] = cf
            cf = cf.astype(f32)
            rp = rp + cf
            colg_ref[:, cols] += jnp.sum(cf.reshape(16, 8, 128), axis=0)
        rowg_ref[rows, :] = jnp.broadcast_to(jnp.sum(rp, axis=1, keepdims=True), (128, 128))

    colg = jnp.sum(colg_ref[...], axis=0, keepdims=True)
    fwd, one, comb, zs = {}, {}, {}, {}

    def push_pair(first):
        rows = [pl.ds(pl.multiple_of(zi(ORDER[i]) * 128, 128), 128) for i in (first, first + 1)]
        lhs = jnp.concatenate([ft[r, :] for r in rows], axis=0)
        prod = jnp.dot(lhs, cbf[...], preferred_element_type=f32)
        for k, i in enumerate((first, first + 1)):
            part = prod[k * 128:(k + 1) * 128]
            part = -2.0 * (part - colg * ct[rows[k], :].astype(f32))
            rs[i] = part.astype(bf16).reshape(4, 32, CENTS)
            sign = 1 if i % 2 == 0 else -1
            fwd[i] = send(rs.at[i, yi(2)], rfwd.at[i], device(dy=sign))
            one[i] = send(rs.at[i, yi(-sign)], rone.at[i], device(dy=-sign))

    def combine(i):
        sign = 1 if i % 2 == 0 else -1
        fwd[i].wait_recv()
        csend[i] = (rs[i, yi(sign)].astype(f32) + rfwd[i].astype(f32)).astype(bf16)
        comb[i] = send(csend.at[i], rcomb.at[i], device(dy=sign))

    def y_total(i):
        one[i].wait_recv()
        comb[i].wait_recv()
        total = rs[i, y].astype(f32) + rone[i].astype(f32) + rcomb[i].astype(f32)
        if ORDER[i] == 0:
            ysum[...] = total
        else:
            zsend[i] = total.astype(bf16)
            zs[i] = send(zsend.at[i], zrecv.at[i], device(dz=ORDER[i]))

    def pull_block(dx):
        rows = chip_rows(dx)
        pull = jnp.dot(cbf[rows, :], cbuf[...], preferred_element_type=f32)
        rg = rowg_ref[rows, :]
        blocks = []
        for h in range(2):
            f = feat[h, rows, :].astype(f32)
            rgw = jnp.concatenate([rg] * 4, axis=1)
            blocks.append(2.0 * (rgw * f - pull[:, h * HALF:(h + 1) * HALF]))
        part = jnp.concatenate(blocks, axis=1)
        psend[dx % NX, 0] = part[0:128].astype(bf16)
        psend[dx % NX, 1] = part[128:256].astype(bf16)
        return send(psend.at[dx % NX, 1 - core], precv.at[dx % NX], device(dc=1))

    pulls, gs = {}, {}

    def pull_sum(dx):
        pulls[dx].wait_recv()
        both = psend[dx, core].astype(f32) + precv[dx].astype(f32)
        if dx == 0:
            pown[...] = both
        else:
            gsend[dx - 1] = both.astype(bf16)
            gs[dx] = send(gsend.at[dx - 1], gx.at[dx - 1], device(dx=dx))

    push_pair(0)
    push_pair(2)
    push_pair(4)
    push_pair(6)
    combine(0)
    pulls[2] = pull_block(2)
    combine(1)
    pulls[1] = pull_block(1)
    combine(2)
    pull_sum(2)
    pulls[3] = pull_block(3)
    combine(3)
    pull_sum(1)
    pulls[0] = pull_block(0)
    pull_sum(3)
    combine(4)
    pull_sum(0)
    for copy in lsy:
        copy.wait_recv()
    lz[z] = (ly[0] + ly[1]) + (ly[2] + ly[3])
    lsz = [send(lz.at[z], lz.at[z], device(dz=d)) for d in range(1, NZ)]
    combine(5)
    combine(6)
    combine(7)
    for i in range(8):
        y_total(i)
    for dx in (1, 3, 2):
        gs[dx].wait_recv()
    gp_ref[...] = pown[...] + gx[0].astype(f32) + gx[1].astype(f32) + gx[2].astype(f32)
    for copy in lsz:
        copy.wait_recv()
    total = lz[0]
    for i in range(1, NZ):
        total = total + lz[i]
    loss_ref[...] = total * (1.0 / DOCS)
    for i in range(7):
        zs[i].wait_recv()
    for h in range(2):
        rows = slice(h * 16, (h + 1) * 16)
        part = ysum[rows, :]
        for i in range(7):
            part = part + zrecv[i, rows, :].astype(f32)
        ysum[rows, :] = part
    xsend[...] = ysum[pl.ds(pl.multiple_of((1 - xh) * 16, 16), 16), :].astype(bf16)
    last = send(xsend, xrecv, device(dx=2))
    gc_ref[:, j_rows] = ysum[pl.ds(pl.multiple_of(xh * 16, 16), 16), :]
    last.wait_recv()
    gc_ref[:, other_rows] = xrecv[...].astype(f32)
    for copy in copies:
        copy.wait_send()


def per_device(embeddings, projection, centroids, target):
    vmem = pltpu.VMEM
    gp, gct, loss = pl.pallas_call(
        body,
        name="cluster_head",
        out_shape=(
            jax.ShapeDtypeStruct((DOCS_DEV, DZ), f32),
            jax.ShapeDtypeStruct((16, 2 * CENTS), f32),
            jax.ShapeDtypeStruct((8, 128), f32),
        ),
        in_specs=[pl.BlockSpec(memory_space=pl.ANY)] * 4,
        out_specs=(pl.BlockSpec(memory_space=vmem),) * 3,
        scratch_shapes=[
            vmem((NZ, NY, 128, HALF), bf16),
            vmem((CHIP_DOCS, DIN), bf16),
            vmem((CENTS, DZ), bf16),
            vmem((DZ, CENTS), bf16),
            vmem((RING_DOCS, CENTS), bf16),
            vmem((2, RING_DOCS, HALF), bf16),
            vmem((DZ, RING_DOCS), bf16),
            vmem((RING_DOCS, CENTS), f32),
            vmem((RING_DOCS, CENTS), bf16),
            vmem((8, 8, RING_DOCS), f32),
            vmem((2, RING_DOCS, 128), f32),
            vmem((RING_DOCS, 128), f32),
            vmem((8, CENTS), f32),
            vmem((8, CENTS), f32),
            vmem((8, 4, 32, CENTS), bf16),
            vmem((8, 32, CENTS), bf16),
            vmem((8, 32, CENTS), bf16),
            vmem((8, 32, CENTS), bf16),
            vmem((8, 32, CENTS), bf16),
            vmem((7, 32, CENTS), bf16),
            vmem((7, 32, CENTS), bf16),
            vmem((32, CENTS), f32),
            vmem((16, CENTS), bf16),
            vmem((16, CENTS), bf16),
            vmem((4, 2, 128, DZ), bf16),
            vmem((128, DZ), f32),
            vmem((4, 128, DZ), bf16),
            vmem((3, 128, DZ), bf16),
            vmem((3, 128, DZ), bf16),
            vmem((NY, 8, 128), f32),
            vmem((NZ, 8, 128), f32),
            pltpu.SemaphoreType.DMA((N_SEM,)),
            pltpu.SemaphoreType.DMA((N_SEM,)),
            pltpu.SemaphoreType.DMA((4,)),
        ],
        compiler_params=pltpu.CompilerParams(
            collective_id=0, has_side_effects=True, vmem_limit_bytes=60 * 2**20
        ),
        cost_estimate=pl.CostEstimate(flops=7_500_000_000, bytes_accessed=9_000_000, transcendentals=3_000_000),
    )(embeddings, projection, centroids, target)
    return gp, gct.T, loss[0, 0]


def solution(mesh):
    placed = (P(("wide", "narrow"), None), P("wide", None), P("narrow", None), P("wide", "narrow"))
    return jax.shard_map(
        per_device,
        mesh=mesh,
        in_specs=placed,
        out_specs=(P(("wide", "narrow"), None), P("narrow", "wide"), P()),
        check_vma=False,
    )
```

```python
import jax
import jax.numpy as jnp
from jax import lax
from jax.experimental import pallas as pl
from jax.experimental.pallas import tpu as pltpu
from jax.sharding import PartitionSpec as P

NZ, NY, NX = 8, 4, 4
DIN, DZ, HALF = 4096, 1024, 512
DOCS_DEV, CHIP_DOCS, RING_DOCS = 128, 256, 1024
CENTS = 1024
DOCS = 32768
SCALE = 64.0
ORDER = (4, 3, -3, 2, -2, 1, -1, 0)
N_SEM = 160
bf16, f32 = jnp.bfloat16, jnp.float32


def body(
    emb, proj, cent, target,
    gp_ref, gc_ref, loss_ref,
    pbuf, ebuf, cbuf, ct, tbuf, feat, ft, kbuf, cbf, stats, ab, rowg_ref, cn_ref, colg_ref,
    rs, rfwd, rone, rcomb, csend, zsend, zrecv, ysum, xsend, xrecv,
    psend, pown, precv, gsend, gx, ly, lz,
    send_sems, recv_sems, local_sems,
):
    wide, narrow = lax.axis_index("wide"), lax.axis_index("narrow")
    z, y, xh = wide // 8, (wide // 2) % 4, wide % 2
    xl, core = narrow // 2, narrow % 2
    x = xh * 2 + xl

    def device(dx=0, dy=0, dz=0, dc=0):
        tx, ty, tz, tc = (x + dx + NX) % NX, (y + dy + NY) % NY, (z + dz + NZ) % NZ, (core + dc) % 2
        return (tz * 8 + ty * 2 + tx // 2, (tx % 2) * 2 + tc)

    def to_device(tx):
        return (z * 8 + y * 2 + tx // 2, (tx % 2) * 2 + core)

    def zi(dz):
        return (z + dz + NZ) % NZ

    def yi(dy):
        return (y + dy + NY) % NY

    def xi(dx):
        return (x + dx + NX) % NX

    copies = []

    def send(src, dst, target_device):
        number = len(copies)
        copy = pltpu.make_async_remote_copy(
            src_ref=src, dst_ref=dst, send_sem=send_sems.at[number], recv_sem=recv_sems.at[number],
            device_id=target_device, device_id_type=pl.DeviceIdType.MESH,
        )
        copy.start()
        copies.append(copy)
        return copy

    locals_ = []

    def local(src, dst):
        copy = pltpu.make_async_copy(src, dst, local_sems.at[len(locals_)])
        copy.start()
        locals_.append(copy)
        return copy

    own_rows = pl.ds(pl.multiple_of(xh * 64, 64), 64)
    own_cols = pl.ds(pl.multiple_of(core * HALF, HALF), HALF)
    l_proj = local(proj.at[:, own_cols], pbuf.at[z, y, own_rows])
    l_emb = local(emb, ebuf.at[pl.ds(pl.multiple_of(core * 128, 128), 128)])
    j_rows = pl.ds(pl.multiple_of(xh * CENTS, CENTS), CENTS)
    other_rows = pl.ds(pl.multiple_of((1 - xh) * CENTS, CENTS), CENTS)
    my_docs = pl.ds(pl.multiple_of(xh * 512, 512), 512)
    l_cent = local(cent.at[j_rows], cbuf)
    l_tgt = local(target.at[:, j_rows], tbuf.at[my_docs])

    ring = [(dx, dc) for dx in range(NX) for dc in range(2) if (dx, dc) != (0, 0)]
    peers = [device(dx=dx, dc=dc) for dx, dc in ring]
    peers += [device(dz=d) for d in range(1, NZ)] + [device(dy=d) for d in range(1, NY)]
    barrier = pltpu.get_barrier_semaphore()
    for peer in peers:
        pl.semaphore_signal(barrier, inc=1, device_id=peer, device_id_type=pl.DeviceIdType.MESH)
    pl.semaphore_wait(barrier, len(peers))

    other_half = pl.ds(pl.multiple_of((1 - xh) * 64, 64), 64)

    def move(part, at_z, at_y, **hop):
        where = pbuf.at[zi(at_z), yi(at_y), own_rows if part == "a" else other_half]
        return send(where, where, device(**hop))

    def move_half(half, at_z, **hop):
        start = pl.multiple_of(xh * 64 + half * 32, 32)
        where = pbuf.at[zi(at_z), y, pl.ds(start, 32)]
        return send(where, where, device(**hop))

    bz, az, ay, by = {}, {}, {}, {}

    def b_own(q):
        bz[q, 1, 1] = move("b", 0, q, dz=1)
        bz[q, -1, 1] = move("b", 0, q, dz=-1)

    def b_y(hop):
        by[hop].wait_recv()
        b_own(2 if hop == 2 else -hop)

    def b_step(step, q):
        for sign in (1, -1):
            if (q, sign, step) in bz:
                bz[q, sign, step].wait_recv()
                if step < 3 or (step == 3 and (sign == 1) == (q in (0, 2))):
                    bz[q, sign, step + 1] = move("b", -sign * step, q, dz=sign)

    def a_y_sends(dz):
        ay[dz, 1] = move("a", dz, 0, dy=1)
        ay[dz, -1] = move("a", dz, 0, dy=-1)

    def a_y_forward(dz):
        if dz % 2 == 0:
            ay[dz, 1].wait_recv()
            ay[dz, 2] = move("a", dz, -1, dy=1)
        else:
            ay[dz, -1].wait_recv()
            ay[dz, 2] = move("a", dz, 1, dy=-1)

    def a_step(step):
        for sign in (1, -1):
            az[sign, step].wait_recv()
            if step < 3:
                az[sign, step + 1] = move("a", -sign * step, 0, dz=sign)
            elif step == 3:
                az[sign, 4] = move_half(0 if sign == 1 else 1, -sign * step, dz=sign)
        a_y_sends(step)
        if step < 4:
            a_y_sends(-step)

    me8 = x * 2 + core

    def target_stats(block):
        rows = pl.ds(pl.multiple_of(block * 128, 128), 128)
        wp = jnp.zeros((128, 128), f32)
        lp = jnp.zeros((128, 128), f32)
        for lane in range(8):
            t = tbuf[rows, lane * 128:(lane + 1) * 128].astype(f32)
            wp = wp + t
            lp = lp + t * jnp.log(t)
        stats[me8, 0:1, rows] = jnp.sum(wp.T, axis=0, keepdims=True)
        stats[me8, 1:2, rows] = jnp.sum(lp.T, axis=0, keepdims=True)

    def centroid_block(j):
        cols = pl.ds(pl.multiple_of(j * 128, 128), 128)
        c = cbuf[cols, :].astype(f32).T
        ct[:, cols] = c.astype(bf16)
        cn_ref[0:1, cols] = jnp.sum(c * c, axis=0, keepdims=True)

    l_proj.wait()
    where = pbuf.at[z, y, own_rows]
    x_swap = send(where, where, to_device(3 - x))
    az[1, 1] = move("a", 0, 0, dz=1)
    az[-1, 1] = move("a", 0, 0, dz=-1)
    a_y_sends(0)
    l_emb.wait()
    mine = ebuf.at[pl.ds(pl.multiple_of(core * 128, 128), 128)]
    e_copy = send(mine, mine, device(dc=1))
    stats[me8] = jnp.zeros((8, RING_DOCS), f32)

    x_swap.wait_recv()
    b_own(0)
    for hop in (1, -1, 2):
        by[hop] = move("b", 0, 0, dy=hop)
    t_copy = send(target.at[:, other_rows], tbuf.at[my_docs], device(dx=2))
    l_cent.wait()
    l_tgt.wait()
    a_step(1)
    a_y_forward(0)
    a_step(2)
    for hop in (1, -1, 2):
        b_y(hop)
    b_step(1, 0)
    a_y_forward(1)
    a_y_forward(-1)
    centroid_block(0)
    a_step(3)
    for q in (-1, 1, 2):
        b_step(1, q)
    b_step(2, 0)
    a_y_forward(2)
    a_y_forward(-2)
    centroid_block(1)
    centroid_block(2)
    a_step(4)
    for q in (-1, 1, 2):
        b_step(2, q)
    b_step(3, 0)
    a_y_forward(3)
    a_y_forward(-3)
    a_y_forward(4)
    centroid_block(3)
    centroid_block(4)
    target_stats(xh * 4)
    for q in (-1, 1, 2):
        b_step(3, q)
    target_stats(xh * 4 + 1)
    centroid_block(5)
    centroid_block(6)
    centroid_block(7)
    target_stats(xh * 4 + 2)
    target_stats(xh * 4 + 3)
    for q in (0, -1, 1, 2):
        b_step(4, q)
    e_copy.wait_recv()
    for dz in (0, 1, -1, 2, -2, 3, -3, 4):
        ay[dz, -1 if dz % 2 == 0 else 1].wait_recv()
        ay[dz, 2].wait_recv()

    def chip_rows(dx):
        return pl.ds(pl.multiple_of(xi(dx) * CHIP_DOCS, CHIP_DOCS), CHIP_DOCS)

    own = jnp.dot(ebuf[...], pbuf[...].reshape(DIN, HALF), preferred_element_type=f32).astype(bf16)
    feat[core, chip_rows(0), :] = own
    fx = {}

    def feat_send(at_x, **hop):
        where = feat.at[core, chip_rows(at_x)]
        return send(where, where, device(**hop))

    fx[1] = feat_send(0, dx=1)
    fx[3] = feat_send(0, dx=-1)
    fc = {0: feat_send(0, dc=1)}
    fx[2] = feat_send(0, dx=2)

    def inner(dx):
        fc[dx].wait_recv()
        rows = chip_rows(dx)
        f0, f1 = feat[0, rows, :], feat[1, rows, :]
        g = jnp.dot(f0, ct[0:HALF, :], preferred_element_type=f32)
        g = g + jnp.dot(f1, ct[HALF:DZ, :], preferred_element_type=f32)
        g0, g1 = f0.astype(f32), f1.astype(f32)
        zn = 1.0 + jnp.sum(g0 * g0 + g1 * g1, axis=1, keepdims=True)
        kp = jnp.zeros((CHIP_DOCS, 128), f32)
        cp = jnp.zeros((CHIP_DOCS, 128), f32)
        for lane in range(8):
            cols = slice(lane * 128, (lane + 1) * 128)
            u = (zn + cn_ref[0:1, cols]) - 2.0 * g[:, cols]
            r = pl.reciprocal(u, approx=True)
            k = r * (2.0 - u * r)
            kbuf[rows, cols] = k
            kp = kp + k
            cp = cp + tbuf[rows, cols].astype(f32) * jnp.log(u)
        stats[me8, 2:3, rows] = jnp.sum(kp.T, axis=0, keepdims=True)
        stats[me8, 3:4, rows] = jnp.sum(cp.T, axis=0, keepdims=True)

    def transpose_features(dx):
        rows = chip_rows(dx)
        ft[0:HALF, rows] = feat[0, rows, :].astype(f32).T.astype(bf16)
        ft[HALF:DZ, rows] = feat[1, rows, :].astype(f32).T.astype(bf16)

    t_copy.wait_recv()

    @pl.loop(0, 4)
    def _(i):
        target_stats((1 - xh) * 4 + i)

    inner(0)
    transpose_features(0)
    for dx in (1, 3, 2):
        fx[dx].wait_recv()
        fc[NX - dx] = feat_send(NX - dx, dc=1)
        inner(NX - dx)
        if dx != 2:
            transpose_features(NX - dx)

    st = []
    for dx, dc in ring:
        st.append(send(stats.at[me8], stats.at[me8], device(dx=dx, dc=dc)))
    transpose_features(2)
    for copy in st:
        copy.wait_recv()
    tot = stats[0]
    for i in range(1, 8):
        tot = tot + stats[i]
    wsum, tlog, ksum, clog = tot[0:1], tot[1:2], tot[2:3], tot[3:4]
    row_loss = (tlog + clog) / wsum - jnp.log(wsum) + jnp.log(ksum)
    ly[y] = jnp.broadcast_to(jnp.sum(row_loss, axis=1, keepdims=True), (8, 128))
    lsy = [send(ly.at[y], ly.at[y], device(dy=d)) for d in range(1, NY)]
    ra, rb = SCALE / wsum, SCALE / ksum
    for block in range(8):
        rows = slice(block * 128, (block + 1) * 128)
        ab[0, rows, :] = jnp.broadcast_to(ra[:, rows], (128, 128)).T
        ab[1, rows, :] = jnp.broadcast_to(rb[:, rows], (128, 128)).T

    colg_ref[...] = jnp.zeros((8, CENTS), f32)

    @pl.loop(0, 8)
    def _(block):
        rows = pl.ds(pl.multiple_of(block * 128, 128), 128)
        a, b = ab[0, rows, :], ab[1, rows, :]
        rp = jnp.zeros((128, 128), f32)
        for lane in range(8):
            cols = slice(lane * 128, (lane + 1) * 128)
            k = kbuf[rows, cols]
            cf = (k * (tbuf[rows, cols].astype(f32) * a - k * b)).astype(bf16)
            cbf[rows, cols] = cf
            cf = cf.astype(f32)
            rp = rp + cf
            colg_ref[:, cols] += jnp.sum(cf.reshape(16, 8, 128), axis=0)
        rowg_ref[rows, :] = jnp.broadcast_to(jnp.sum(rp, axis=1, keepdims=True), (128, 128))

    colg = jnp.sum(colg_ref[...], axis=0, keepdims=True)
    fwd, one, comb, zs = {}, {}, {}, {}

    def push_pair(first):
        rows = [pl.ds(pl.multiple_of(zi(ORDER[i]) * 128, 128), 128) for i in (first, first + 1)]
        lhs = jnp.concatenate([ft[r, :] for r in rows], axis=0)
        prod = jnp.dot(lhs, cbf[...], preferred_element_type=f32)
        for k, i in enumerate((first, first + 1)):
            part = prod[k * 128:(k + 1) * 128]
            part = -2.0 * (part - colg * ct[rows[k], :].astype(f32))
            rs[i] = part.astype(bf16).reshape(4, 32, CENTS)
            sign = 1 if i % 2 == 0 else -1
            fwd[i] = send(rs.at[i, yi(2)], rfwd.at[i], device(dy=sign))
            one[i] = send(rs.at[i, yi(-sign)], rone.at[i], device(dy=-sign))

    def combine(i):
        sign = 1 if i % 2 == 0 else -1
        fwd[i].wait_recv()
        csend[i] = (rs[i, yi(sign)].astype(f32) + rfwd[i].astype(f32)).astype(bf16)
        comb[i] = send(csend.at[i], rcomb.at[i], device(dy=sign))

    def y_total(i):
        one[i].wait_recv()
        comb[i].wait_recv()
        total = rs[i, y].astype(f32) + rone[i].astype(f32) + rcomb[i].astype(f32)
        if ORDER[i] == 0:
            ysum[...] = total
        else:
            zsend[i] = total.astype(bf16)
            zs[i] = send(zsend.at[i], zrecv.at[i], device(dz=ORDER[i]))

    def pull_block(dx):
        rows = chip_rows(dx)
        pull = jnp.dot(cbf[rows, :], cbuf[...], preferred_element_type=f32)
        rg = rowg_ref[rows, :]
        blocks = []
        for h in range(2):
            f = feat[h, rows, :].astype(f32)
            rgw = jnp.concatenate([rg] * 4, axis=1)
            blocks.append(2.0 * (rgw * f - pull[:, h * HALF:(h + 1) * HALF]))
        part = jnp.concatenate(blocks, axis=1)
        psend[dx % NX, 0] = part[0:128].astype(bf16)
        psend[dx % NX, 1] = part[128:256].astype(bf16)
        return send(psend.at[dx % NX, 1 - core], precv.at[dx % NX], device(dc=1))

    pulls, gs = {}, {}

    def pull_sum(dx):
        pulls[dx].wait_recv()
        both = psend[dx, core].astype(f32) + precv[dx].astype(f32)
        if dx == 0:
            pown[...] = both
        else:
            gsend[dx - 1] = both.astype(bf16)
            gs[dx] = send(gsend.at[dx - 1], gx.at[dx - 1], device(dx=dx))

    push_pair(0)
    push_pair(2)
    pulls[2] = pull_block(2)
    combine(0)
    combine(1)
    push_pair(4)
    pulls[1] = pull_block(1)
    pull_sum(2)
    combine(2)
    combine(3)
    push_pair(6)
    pulls[3] = pull_block(3)
    pull_sum(1)
    y_total(0)
    y_total(1)
    pulls[0] = pull_block(0)
    pull_sum(3)
    combine(4)
    combine(5)
    for copy in lsy:
        copy.wait_recv()
    lz[z] = (ly[0] + ly[1]) + (ly[2] + ly[3])
    lsz = [send(lz.at[z], lz.at[z], device(dz=d)) for d in range(1, NZ)]
    y_total(2)
    y_total(3)
    pull_sum(0)
    combine(6)
    combine(7)
    y_total(4)
    y_total(5)
    y_total(6)
    y_total(7)
    for dx in (1, 3, 2):
        gs[dx].wait_recv()
    gp_ref[...] = pown[...] + gx[0].astype(f32) + gx[1].astype(f32) + gx[2].astype(f32)
    for copy in lsz:
        copy.wait_recv()
    total = lz[0]
    for i in range(1, NZ):
        total = total + lz[i]
    loss_ref[...] = total * (1.0 / DOCS)
    for i in range(7):
        zs[i].wait_recv()
    for h in range(2):
        rows = slice(h * 16, (h + 1) * 16)
        part = ysum[rows, :]
        for i in range(7):
            part = part + zrecv[i, rows, :].astype(f32)
        ysum[rows, :] = part
    xsend[...] = ysum[pl.ds(pl.multiple_of((1 - xh) * 16, 16), 16), :].astype(bf16)
    last = send(xsend, xrecv, device(dx=2))
    gc_ref[:, j_rows] = ysum[pl.ds(pl.multiple_of(xh * 16, 16), 16), :]
    last.wait_recv()
    gc_ref[:, other_rows] = xrecv[...].astype(f32)
    for copy in copies:
        copy.wait_send()


def hand_over(gp, gc, loss, gp_out, gc_out, loss_out):
    gp_out[...] = gp[...]
    gc_out[...] = gc[...]
    loss_out[0, 0] = loss[0, 0]


def per_device(embeddings, projection, centroids, target):
    vmem = pltpu.VMEM
    outs = pl.pallas_call(
        body,
        name="cluster_head",
        out_shape=(
            jax.ShapeDtypeStruct((DOCS_DEV, DZ), f32),
            jax.ShapeDtypeStruct((16, 2 * CENTS), f32),
            jax.ShapeDtypeStruct((8, 128), f32),
        ),
        in_specs=[pl.BlockSpec(memory_space=pl.ANY)] * 4,
        out_specs=(pl.BlockSpec(memory_space=vmem),) * 3,
        scratch_shapes=[
            vmem((NZ, NY, 128, HALF), bf16),
            vmem((CHIP_DOCS, DIN), bf16),
            vmem((CENTS, DZ), bf16),
            vmem((DZ, CENTS), bf16),
            vmem((RING_DOCS, CENTS), bf16),
            vmem((2, RING_DOCS, HALF), bf16),
            vmem((DZ, RING_DOCS), bf16),
            vmem((RING_DOCS, CENTS), f32),
            vmem((RING_DOCS, CENTS), bf16),
            vmem((8, 8, RING_DOCS), f32),
            vmem((2, RING_DOCS, 128), f32),
            vmem((RING_DOCS, 128), f32),
            vmem((8, CENTS), f32),
            vmem((8, CENTS), f32),
            vmem((8, 4, 32, CENTS), bf16),
            vmem((8, 32, CENTS), bf16),
            vmem((8, 32, CENTS), bf16),
            vmem((8, 32, CENTS), bf16),
            vmem((8, 32, CENTS), bf16),
            vmem((7, 32, CENTS), bf16),
            vmem((7, 32, CENTS), bf16),
            vmem((32, CENTS), f32),
            vmem((16, CENTS), bf16),
            vmem((16, CENTS), bf16),
            vmem((4, 2, 128, DZ), bf16),
            vmem((128, DZ), f32),
            vmem((4, 128, DZ), bf16),
            vmem((3, 128, DZ), bf16),
            vmem((3, 128, DZ), bf16),
            vmem((NY, 8, 128), f32),
            vmem((NZ, 8, 128), f32),
            pltpu.SemaphoreType.DMA((N_SEM,)),
            pltpu.SemaphoreType.DMA((N_SEM,)),
            pltpu.SemaphoreType.DMA((4,)),
        ],
        compiler_params=pltpu.CompilerParams(
            collective_id=0, has_side_effects=True, vmem_limit_bytes=60 * 2**20
        ),
        cost_estimate=pl.CostEstimate(flops=7_500_000_000, bytes_accessed=9_000_000, transcendentals=3_000_000),
    )(embeddings, projection, centroids, target)
    gp, gct, loss = pl.pallas_call(
        hand_over,
        name="hand_over",
        out_shape=(
            jax.ShapeDtypeStruct((DOCS_DEV, DZ), f32),
            jax.ShapeDtypeStruct((16, 2 * CENTS), f32),
            jax.ShapeDtypeStruct((1, 1), f32),
        ),
        in_specs=[pl.BlockSpec(memory_space=vmem)] * 3,
        out_specs=(pl.BlockSpec(memory_space=vmem),) * 2 + (pl.BlockSpec(memory_space=pltpu.SMEM),),
    )(*outs)
    return gp, gct.T, loss.reshape(())


def solution(mesh):
    placed = (P(("wide", "narrow"), None), P("wide", None), P("narrow", None), P("wide", "narrow"))
    return jax.shard_map(
        per_device,
        mesh=mesh,
        in_specs=placed,
        out_specs=(P(("wide", "narrow"), None), P("narrow", "wide"), P()),
        check_vma=False,
    )
```

```python
import jax
import jax.numpy as jnp
from jax import lax
from jax.experimental import pallas as pl
from jax.experimental.pallas import tpu as pltpu
from jax.sharding import PartitionSpec as P

NZ, NY, NX = 8, 4, 4
DIN, DZ, HALF, QUARTER = 4096, 1024, 512, 256
DOCS_DEV, CHIP_DOCS, RING_DOCS = 128, 256, 1024
CENTS = 1024
DOCS = 32768
SCALE = 64.0
Y_FIRST, Z_FIRST = 896, 128
ORDER = (4, 3, -3, 2, -2, 1, -1, 0)
N_SEM = 288
bf16, f32 = jnp.bfloat16, jnp.float32


def body(
    emb, proj, cent, target,
    gp_ref, gc_ref, loss_ref,
    pbuf, ebuf, cbuf, ct, tbuf, feat, ft, kbuf, cbf, early, late, ab, rowg_ref, cn_ref, colg_ref,
    rs, rfwd, rone, rcomb, csend, zsend, zrecv, zb, zbr, ybs, ybr, ysum, xsend, xrecv,
    psend, pown, precv, gsend, gx, ly, lz,
    send_sems, recv_sems, local_sems,
):
    wide, narrow = lax.axis_index("wide"), lax.axis_index("narrow")
    z, y, xh = wide // 8, (wide // 2) % 4, wide % 2
    xl, core = narrow // 2, narrow % 2
    x = xh * 2 + xl

    def device(dx=0, dy=0, dz=0, dc=0):
        tx, ty, tz, tc = (x + dx + NX) % NX, (y + dy + NY) % NY, (z + dz + NZ) % NZ, (core + dc) % 2
        return (tz * 8 + ty * 2 + tx // 2, (tx % 2) * 2 + tc)

    def to_device(tx):
        return (z * 8 + y * 2 + tx // 2, (tx % 2) * 2 + core)

    def zi(dz):
        return (z + dz + NZ) % NZ

    def yi(dy):
        return (y + dy + NY) % NY

    def xi(dx):
        return (x + dx + NX) % NX

    copies = []

    def send(src, dst, target_device):
        number = len(copies)
        copy = pltpu.make_async_remote_copy(
            src_ref=src, dst_ref=dst, send_sem=send_sems.at[number], recv_sem=recv_sems.at[number],
            device_id=target_device, device_id_type=pl.DeviceIdType.MESH,
        )
        copy.start()
        copies.append(copy)
        return copy

    locals_ = []

    def local(src, dst):
        copy = pltpu.make_async_copy(src, dst, local_sems.at[len(locals_)])
        copy.start()
        locals_.append(copy)
        return copy

    own_rows = pl.ds(pl.multiple_of(xh * 64, 64), 64)
    l_proj = []
    for r in range(2):
        cols = pl.ds(pl.multiple_of(core * HALF + r * QUARTER, QUARTER), QUARTER)
        l_proj.append(local(proj.at[:, cols], pbuf.at[r, z, y, own_rows]))
    l_emb = local(emb, ebuf.at[pl.ds(pl.multiple_of(core * 128, 128), 128)])
    j_rows = pl.ds(pl.multiple_of(xh * CENTS, CENTS), CENTS)
    other_rows = pl.ds(pl.multiple_of((1 - xh) * CENTS, CENTS), CENTS)
    my_docs = pl.ds(pl.multiple_of(xh * 512, 512), 512)
    l_cent = local(cent.at[j_rows], cbuf)
    l_tgt = local(target.at[:, j_rows], tbuf.at[my_docs])

    ring = [(dx, dc) for dx in range(NX) for dc in range(2) if (dx, dc) != (0, 0)]
    peers = [device(dx=dx, dc=dc) for dx, dc in ring]
    peers += [device(dz=d) for d in range(1, NZ)] + [device(dy=d) for d in range(1, NY)]
    barrier = pltpu.get_barrier_semaphore()
    for peer in peers:
        pl.semaphore_signal(barrier, inc=1, device_id=peer, device_id_type=pl.DeviceIdType.MESH)
    pl.semaphore_wait(barrier, len(peers))

    other_half = pl.ds(pl.multiple_of((1 - xh) * 64, 64), 64)

    class Gather:
        def __init__(self, r):
            self.buf = pbuf.at[r]
            self.bz, self.az, self.ay, self.by = {}, {}, {}, {}

        def move(self, part, at_z, at_y, **hop):
            where = self.buf.at[zi(at_z), yi(at_y), own_rows if part == "a" else other_half]
            return send(where, where, device(**hop))

        def move_half(self, half, at_z, **hop):
            start = pl.multiple_of(xh * 64 + half * 32, 32)
            where = self.buf.at[zi(at_z), y, pl.ds(start, 32)]
            return send(where, where, device(**hop))

        def b_own(self, q):
            for sign in (1, -1):
                self.bz[q, sign, 1] = self.move("b", 0, q, dz=sign)

        def b_y(self, hop):
            self.by[hop].wait_recv()
            self.b_own(2 if hop == 2 else -hop)

        def b_step(self, step, q):
            for sign in (1, -1):
                if (q, sign, step) in self.bz:
                    self.bz[q, sign, step].wait_recv()
                    if step < 3 or (step == 3 and (sign == 1) == (q in (0, 2))):
                        self.bz[q, sign, step + 1] = self.move("b", -sign * step, q, dz=sign)

        def a_y_sends(self, dz):
            for sign in (1, -1):
                self.ay[dz, sign] = self.move("a", dz, 0, dy=sign)

        def a_y_forward(self, dz):
            sign = 1 if dz % 2 == 0 else -1
            self.ay[dz, sign].wait_recv()
            self.ay[dz, 2] = self.move("a", dz, -sign, dy=sign)

        def a_step(self, step):
            for sign in (1, -1):
                self.az[sign, step].wait_recv()
                if step < 3:
                    self.az[sign, step + 1] = self.move("a", -sign * step, 0, dz=sign)
                elif step == 3:
                    self.az[sign, 4] = self.move_half(0 if sign == 1 else 1, -sign * step, dz=sign)
            self.a_y_sends(step)
            if step < 4:
                self.a_y_sends(-step)

        def group(self, g):
            if g == 0:
                where = self.buf.at[z, y, own_rows]
                self.x_swap = send(where, where, to_device(3 - x))
                for sign in (1, -1):
                    self.az[sign, 1] = self.move("a", 0, 0, dz=sign)
                self.a_y_sends(0)
            elif g == 1:
                self.x_swap.wait_recv()
                self.b_own(0)
                for hop in (1, -1, 2):
                    self.by[hop] = self.move("b", 0, 0, dy=hop)
            elif g in (2, 4, 7, 10):
                self.a_step({2: 1, 4: 2, 7: 3, 10: 4}[g])
            elif g == 3:
                self.a_y_forward(0)
            elif g == 5:
                for hop in (1, -1, 2):
                    self.b_y(hop)
                self.b_step(1, 0)
            elif g in (6, 9, 12):
                step = g // 3 - 1
                self.a_y_forward(step)
                self.a_y_forward(-step)
                if step == 3:
                    self.a_y_forward(4)
            elif g in (8, 11, 13):
                step = {8: 1, 11: 2, 13: 3}[g]
                for q in (-1, 1, 2):
                    self.b_step(step, q)
                if step < 3:
                    self.b_step(step + 1, 0)
            else:
                for q in (0, -1, 1, 2):
                    self.b_step(4, q)
                for dz in (0, 1, -1, 2, -2, 3, -3, 4):
                    self.ay[dz, -1 if dz % 2 == 0 else 1].wait_recv()
                    self.ay[dz, 2].wait_recv()

    me8 = x * 2 + core

    def put_stat(stat, block, partial):
        cols = pl.ds(pl.multiple_of((block % 4) * 128, 128), 128)
        early[me8, block // 4, stat:stat + 1, cols] = jnp.sum(partial.T, axis=0, keepdims=True)

    def target_stats(block):
        rows = pl.ds(pl.multiple_of(block * 128, 128), 128)
        wp = jnp.zeros((128, 128), f32)
        lp = jnp.zeros((128, 128), f32)
        for lane in range(8):
            t = tbuf[rows, lane * 128:(lane + 1) * 128].astype(f32)
            wp = wp + t
            lp = lp + t * jnp.log(t)
        put_stat(0, block, wp)
        put_stat(1, block, lp)

    def centroid_block(j):
        cols = pl.ds(pl.multiple_of(j * 128, 128), 128)
        c = cbuf[cols, :].astype(f32).T
        ct[:, cols] = c.astype(bf16)
        cn_ref[0:1, cols] = jnp.sum(c * c, axis=0, keepdims=True)

    rounds = [Gather(0), Gather(1)]
    fx, fc = {}, {}

    def chip_rows(dx):
        return pl.ds(pl.multiple_of(xi(dx) * CHIP_DOCS, CHIP_DOCS), CHIP_DOCS)

    def feat_send(r, at_x, **hop):
        where = feat.at[2 * core + r, chip_rows(at_x)]
        return send(where, where, device(**hop))

    def finish_round(r):
        rounds[r].group(14)
        if r == 0:
            e_copy.wait_recv()
        own = jnp.dot(ebuf[...], pbuf[r].reshape(DIN, QUARTER), preferred_element_type=f32)
        feat[2 * core + r, chip_rows(0), :] = own.astype(bf16)
        fx[r, 1] = feat_send(r, 0, dx=1)
        fx[r, 3] = feat_send(r, 0, dx=-1)
        fc[r, 0] = feat_send(r, 0, dc=1)
        fx[r, 2] = feat_send(r, 0, dx=2)

    l_proj[0].wait()
    rounds[0].group(0)
    l_emb.wait()
    mine = ebuf.at[pl.ds(pl.multiple_of(core * 128, 128), 128)]
    e_copy = send(mine, mine, device(dc=1))
    early[me8] = jnp.zeros((2, 4, 512), f32)
    late[me8] = jnp.zeros((8, 128), f32)
    l_proj[1].wait()
    rounds[1].group(0)
    rounds[0].group(1)
    rounds[1].group(1)
    t_copy = send(target.at[:, other_rows], tbuf.at[my_docs], device(dx=2))
    l_cent.wait()
    l_tgt.wait()
    rounds[0].group(2)
    rounds[0].group(3)
    rounds[0].group(4)
    rounds[0].group(5)
    rounds[0].group(6)
    rounds[1].group(2)
    centroid_block(0)
    rounds[0].group(7)
    rounds[1].group(3)
    rounds[0].group(8)
    centroid_block(1)
    rounds[1].group(4)
    rounds[0].group(9)
    rounds[1].group(5)
    centroid_block(2)
    rounds[0].group(10)
    rounds[1].group(6)
    rounds[0].group(11)
    centroid_block(3)
    rounds[1].group(7)
    rounds[0].group(12)
    rounds[1].group(8)
    centroid_block(4)
    rounds[0].group(13)
    rounds[1].group(9)
    rounds[1].group(10)
    centroid_block(5)
    rounds[1].group(11)
    rounds[1].group(12)
    finish_round(0)
    rounds[1].group(13)
    centroid_block(6)
    centroid_block(7)
    target_stats(xh * 4 + 0)
    target_stats(xh * 4 + 1)
    target_stats(xh * 4 + 2)
    target_stats(xh * 4 + 3)
    finish_round(1)

    def inner(dx):
        fc[0, dx].wait_recv()
        fc[1, dx].wait_recv()
        rows = chip_rows(dx)
        parts = [feat[i, rows, :] for i in range(4)]
        f = jnp.concatenate(parts, axis=1)
        g = jnp.dot(f, ct[...], preferred_element_type=f32)
        sq = jnp.zeros((CHIP_DOCS, QUARTER), f32)
        for part in parts:
            sq = sq + part.astype(f32) * part.astype(f32)
        zn = 1.0 + jnp.sum(sq, axis=1, keepdims=True)
        kp = jnp.zeros((CHIP_DOCS, 128), f32)
        cp = jnp.zeros((CHIP_DOCS, 128), f32)
        for lane in range(8):
            cols = slice(lane * 128, (lane + 1) * 128)
            u = (zn + cn_ref[0:1, cols]) - 2.0 * g[:, cols]
            r = pl.reciprocal(u, approx=True)
            k = r * (2.0 - u * r)
            kbuf[rows, cols] = k
            kp = kp + k
            cp = cp + tbuf[rows, cols].astype(f32) * jnp.log(u)
        for h in range(2):
            half = slice(h * 128, (h + 1) * 128)
            if dx == 2:
                late[me8, h:h + 1, :] = jnp.sum(kp[half].T, axis=0, keepdims=True)
                late[me8, 2 + h:3 + h, :] = jnp.sum(cp[half].T, axis=0, keepdims=True)
            else:
                put_stat(2, xi(dx) * 2 + h, kp[half])
                put_stat(3, xi(dx) * 2 + h, cp[half])

    def transpose_features(dx):
        rows = chip_rows(dx)
        for i in range(4):
            ft[i * QUARTER:(i + 1) * QUARTER, rows] = feat[i, rows, :].astype(f32).T.astype(bf16)

    t_copy.wait_recv()

    @pl.loop(0, 4)
    def _(i):
        target_stats((1 - xh) * 4 + i)

    def pass_on(r, dx):
        fx[r, dx].wait_recv()
        fc[r, NX - dx] = feat_send(r, NX - dx, dc=1)

    for dx in (1, 3, 2):
        pass_on(0, dx)
    inner(0)
    transpose_features(0)
    pass_on(1, 1)
    pass_on(1, 3)
    inner(1)
    pass_on(1, 2)
    inner(3)
    st = [send(early.at[me8], early.at[me8], device(dx=dx, dc=dc)) for dx, dc in ring]
    inner(2)
    st += [send(late.at[me8], late.at[me8], device(dx=dx, dc=dc)) for dx, dc in ring]
    for dx in (1, 3, 2):
        transpose_features(dx)
    for copy in st:
        copy.wait_recv()

    def lanes(parts):
        return jnp.concatenate(parts, axis=1)

    def totals(stat):
        tot = jnp.zeros((1, RING_DOCS), f32)
        for i in range(8):
            tot = tot + lanes([early[i, 0, stat:stat + 1, :], early[i, 1, stat:stat + 1, :]])
        if stat < 2:
            return tot
        for c in range(2):
            tot = tot + lanes([
                late[2 * ((b // 2 + 2) % 4) + c, (stat - 2) * 2 + b % 2:(stat - 2) * 2 + b % 2 + 1, :]
                for b in range(8)
            ])
        return tot

    wsum, ksum = totals(0), totals(2)
    ra, rb = SCALE / wsum, SCALE / ksum
    for block in range(8):
        rows = slice(block * 128, (block + 1) * 128)
        ab[0, rows, :] = jnp.broadcast_to(ra[:, rows], (128, 128)).T
        ab[1, rows, :] = jnp.broadcast_to(rb[:, rows], (128, 128)).T

    colg_ref[...] = jnp.zeros((8, CENTS), f32)

    @pl.loop(0, 8)
    def _(block):
        rows = pl.ds(pl.multiple_of(block * 128, 128), 128)
        a, b = ab[0, rows, :], ab[1, rows, :]
        rp = jnp.zeros((128, 128), f32)
        for lane in range(8):
            cols = slice(lane * 128, (lane + 1) * 128)
            k = kbuf[rows, cols]
            cf = (k * (tbuf[rows, cols].astype(f32) * a - k * b)).astype(bf16)
            cbf[rows, cols] = cf
            cf = cf.astype(f32)
            rp = rp + cf
            colg_ref[:, cols] += jnp.sum(cf.reshape(16, 8, 128), axis=0)
        rowg_ref[rows, :] = jnp.broadcast_to(jnp.sum(rp, axis=1, keepdims=True), (128, 128))

    colg = jnp.sum(colg_ref[...], axis=0, keepdims=True)
    fwd, one, comb, zs, zfirst, yb = {}, {}, {}, {}, {}, {}

    def push_pair(first):
        rows = [pl.ds(pl.multiple_of(zi(ORDER[i]) * 128, 128), 128) for i in (first, first + 1)]
        lhs = jnp.concatenate([ft[r, :] for r in rows], axis=0)
        prod = jnp.dot(lhs, cbf[...], preferred_element_type=f32)
        for k, i in enumerate((first, first + 1)):
            part = prod[k * 128:(k + 1) * 128]
            part = -2.0 * (part - colg * ct[rows[k], :].astype(f32))
            part = part.astype(bf16)
            rs[i] = part[:, :Y_FIRST].reshape(4, 32, Y_FIRST)
            zb[i] = part[:, Y_FIRST:]
            sign = 1 if i % 2 == 0 else -1
            fwd[i] = send(rs.at[i, yi(2)], rfwd.at[i], device(dy=sign))
            one[i] = send(rs.at[i, yi(-sign)], rone.at[i], device(dy=-sign))
            if ORDER[i] != 0:
                zfirst[i] = send(zb.at[i], zbr.at[i], device(dz=ORDER[i]))

    def combine(i):
        sign = 1 if i % 2 == 0 else -1
        fwd[i].wait_recv()
        csend[i] = (rs[i, yi(sign)].astype(f32) + rfwd[i].astype(f32)).astype(bf16)
        comb[i] = send(csend.at[i], rcomb.at[i], device(dy=sign))

    def y_total(i):
        one[i].wait_recv()
        comb[i].wait_recv()
        total = rs[i, y].astype(f32) + rone[i].astype(f32) + rcomb[i].astype(f32)
        if ORDER[i] == 0:
            ysum[:, :Y_FIRST] = total
        else:
            zsend[i] = total.astype(bf16)
            zs[i] = send(zsend.at[i], zrecv.at[i], device(dz=ORDER[i]))

    def z_first_total():
        total = zb[7].astype(f32)
        for i in range(7):
            zfirst[i].wait_recv()
            total = total + zbr[i].astype(f32)
        ybs[...] = total.astype(bf16).reshape(4, 32, Z_FIRST)
        for d in range(1, NY):
            yb[d] = send(ybs.at[yi(d)], ybr.at[d - 1], device(dy=d))

    def pull_block(dx):
        rows = chip_rows(dx)
        pull = jnp.dot(cbf[rows, :], cbuf[...], preferred_element_type=f32)
        rg = rowg_ref[rows, :]
        blocks = []
        for h in range(4):
            f = feat[h, rows, :].astype(f32)
            rgw = jnp.concatenate([rg] * 2, axis=1)
            blocks.append(2.0 * (rgw * f - pull[:, h * QUARTER:(h + 1) * QUARTER]))
        part = jnp.concatenate(blocks, axis=1)
        psend[dx % NX, 0] = part[0:128].astype(bf16)
        psend[dx % NX, 1] = part[128:256].astype(bf16)
        return send(psend.at[dx % NX, 1 - core], precv.at[dx % NX], device(dc=1))

    pulls, gs = {}, {}

    def pull_sum(dx):
        pulls[dx].wait_recv()
        both = psend[dx, core].astype(f32) + precv[dx].astype(f32)
        if dx == 0:
            pown[...] = both
        else:
            gsend[dx - 1] = both.astype(bf16)
            gs[dx] = send(gsend.at[dx - 1], gx.at[dx - 1], device(dx=dx))

    push_pair(0)
    push_pair(2)
    tlog, clog = totals(1), totals(3)
    row_loss = (tlog + clog) / wsum - jnp.log(wsum) + jnp.log(ksum)
    ly[y] = jnp.broadcast_to(jnp.sum(row_loss, axis=1, keepdims=True), (8, 128))
    lsy = [send(ly.at[y], ly.at[y], device(dy=d)) for d in range(1, NY)]
    pulls[2] = pull_block(2)
    combine(0)
    combine(1)
    push_pair(4)
    pulls[1] = pull_block(1)
    pull_sum(2)
    combine(2)
    combine(3)
    push_pair(6)
    pulls[3] = pull_block(3)
    pull_sum(1)
    z_first_total()
    y_total(0)
    y_total(1)
    pulls[0] = pull_block(0)
    pull_sum(3)
    combine(4)
    combine(5)
    for copy in lsy:
        copy.wait_recv()
    lz[z] = (ly[0] + ly[1]) + (ly[2] + ly[3])
    lsz = [send(lz.at[z], lz.at[z], device(dz=d)) for d in range(1, NZ)]
    y_total(2)
    y_total(3)
    pull_sum(0)
    combine(6)
    combine(7)
    y_total(4)
    y_total(5)
    y_total(6)
    y_total(7)
    for dx in (1, 3, 2):
        gs[dx].wait_recv()
    gp_ref[...] = pown[...] + gx[0].astype(f32) + gx[1].astype(f32) + gx[2].astype(f32)
    for copy in lsz:
        copy.wait_recv()
    total = lz[0]
    for i in range(1, NZ):
        total = total + lz[i]
    loss_ref[...] = total * (1.0 / DOCS)
    for d in range(1, NY):
        yb[d].wait_recv()
    for i in range(7):
        zs[i].wait_recv()
    for h in range(2):
        rows = slice(h * 16, (h + 1) * 16)
        part = ysum[rows, :Y_FIRST]
        for i in range(7):
            part = part + zrecv[i, rows, :].astype(f32)
        ysum[rows, :Y_FIRST] = part
        part = ybs[y, rows, :].astype(f32)
        for i in range(3):
            part = part + ybr[i, rows, :].astype(f32)
        ysum[rows, Y_FIRST:] = part
    xsend[...] = ysum[pl.ds(pl.multiple_of((1 - xh) * 16, 16), 16), :].astype(bf16)
    last = send(xsend, xrecv, device(dx=2))
    gc_ref[:, j_rows] = ysum[pl.ds(pl.multiple_of(xh * 16, 16), 16), :]
    last.wait_recv()
    gc_ref[:, other_rows] = xrecv[...].astype(f32)
    for copy in copies:
        copy.wait_send()


def hand_over(gp, gc, loss, gp_out, gc_out, loss_out):
    gp_out[...] = gp[...]
    gc_out[...] = gc[...]
    loss_out[0, 0] = loss[0, 0]


def per_device(embeddings, projection, centroids, target):
    vmem = pltpu.VMEM
    outs = pl.pallas_call(
        body,
        name="cluster_head",
        out_shape=(
            jax.ShapeDtypeStruct((DOCS_DEV, DZ), f32),
            jax.ShapeDtypeStruct((16, 2 * CENTS), f32),
            jax.ShapeDtypeStruct((8, 128), f32),
        ),
        in_specs=[pl.BlockSpec(memory_space=pl.ANY)] * 4,
        out_specs=(pl.BlockSpec(memory_space=vmem),) * 3,
        scratch_shapes=[
            vmem((2, NZ, NY, 128, QUARTER), bf16),
            vmem((CHIP_DOCS, DIN), bf16),
            vmem((CENTS, DZ), bf16),
            vmem((DZ, CENTS), bf16),
            vmem((RING_DOCS, CENTS), bf16),
            vmem((4, RING_DOCS, QUARTER), bf16),
            vmem((DZ, RING_DOCS), bf16),
            vmem((RING_DOCS, CENTS), f32),
            vmem((RING_DOCS, CENTS), bf16),
            vmem((8, 2, 4, 512), f32),
            vmem((8, 8, 128), f32),
            vmem((2, RING_DOCS, 128), f32),
            vmem((RING_DOCS, 128), f32),
            vmem((8, CENTS), f32),
            vmem((8, CENTS), f32),
            vmem((8, 4, 32, Y_FIRST), bf16),
            vmem((8, 32, Y_FIRST), bf16),
            vmem((8, 32, Y_FIRST), bf16),
            vmem((8, 32, Y_FIRST), bf16),
            vmem((8, 32, Y_FIRST), bf16),
            vmem((7, 32, Y_FIRST), bf16),
            vmem((7, 32, Y_FIRST), bf16),
            vmem((8, 128, Z_FIRST), bf16),
            vmem((7, 128, Z_FIRST), bf16),
            vmem((4, 32, Z_FIRST), bf16),
            vmem((3, 32, Z_FIRST), bf16),
            vmem((32, CENTS), f32),
            vmem((16, CENTS), bf16),
            vmem((16, CENTS), bf16),
            vmem((4, 2, 128, DZ), bf16),
            vmem((128, DZ), f32),
            vmem((4, 128, DZ), bf16),
            vmem((3, 128, DZ), bf16),
            vmem((3, 128, DZ), bf16),
            vmem((NY, 8, 128), f32),
            vmem((NZ, 8, 128), f32),
            pltpu.SemaphoreType.DMA((N_SEM,)),
            pltpu.SemaphoreType.DMA((N_SEM,)),
            pltpu.SemaphoreType.DMA((5,)),
        ],
        compiler_params=pltpu.CompilerParams(
            collective_id=0, has_side_effects=True, vmem_limit_bytes=60 * 2**20
        ),
        cost_estimate=pl.CostEstimate(flops=7_500_000_000, bytes_accessed=9_000_000, transcendentals=3_000_000),
    )(embeddings, projection, centroids, target)
    gp, gct, loss = pl.pallas_call(
        hand_over,
        name="hand_over",
        out_shape=(
            jax.ShapeDtypeStruct((DOCS_DEV, DZ), f32),
            jax.ShapeDtypeStruct((16, 2 * CENTS), f32),
            jax.ShapeDtypeStruct((1, 1), f32),
        ),
        in_specs=[pl.BlockSpec(memory_space=vmem)] * 3,
        out_specs=(pl.BlockSpec(memory_space=vmem),) * 2 + (pl.BlockSpec(memory_space=pltpu.SMEM),),
    )(*outs)
    return gp, gct.T, loss.reshape(())


def solution(mesh):
    placed = (P(("wide", "narrow"), None), P("wide", None), P("narrow", None), P("wide", "narrow"))
    return jax.shard_map(
        per_device,
        mesh=mesh,
        in_specs=placed,
        out_specs=(P(("wide", "narrow"), None), P("narrow", "wide"), P()),
        check_vma=False,
    )
```

```python
import jax
import jax.numpy as jnp
from jax import lax
from jax.experimental import pallas as pl
from jax.experimental.pallas import tpu as pltpu
from jax.sharding import PartitionSpec as P

NZ, NY, NX = 8, 4, 4
DIN, DZ, HALF, QUARTER = 4096, 1024, 512, 256
DOCS_DEV, CHIP_DOCS, RING_DOCS = 128, 256, 1024
CENTS = 1024
DOCS = 32768
SCALE = 64.0
Y_FIRST, Z_FIRST = 896, 128
ORDER = (4, 3, -3, 2, -2, 1, -1, 0)
N_SEM = 288
bf16, f32 = jnp.bfloat16, jnp.float32


def body(
    emb, proj, cent, target,
    gp_ref, gc_ref, loss_ref,
    pbuf, ebuf, cbuf, ct, tbuf, feat, ft, kbuf, cbf, early, late, ab, rowg_ref, cn_ref, colg_ref,
    rs, rfwd, rone, rcomb, csend, zsend, zrecv, zb, zbr, ybs, ybr, ysum, xsend, xrecv,
    psend, pown, precv, gsend, gx, ly, lz,
    send_sems, recv_sems, local_sems,
):
    wide, narrow = lax.axis_index("wide"), lax.axis_index("narrow")
    z, y, xh = wide // 8, (wide // 2) % 4, wide % 2
    xl, core = narrow // 2, narrow % 2
    x = xh * 2 + xl

    def device(dx=0, dy=0, dz=0, dc=0):
        tx, ty, tz, tc = (x + dx + NX) % NX, (y + dy + NY) % NY, (z + dz + NZ) % NZ, (core + dc) % 2
        return (tz * 8 + ty * 2 + tx // 2, (tx % 2) * 2 + tc)

    def to_device(tx):
        return (z * 8 + y * 2 + tx // 2, (tx % 2) * 2 + core)

    def zi(dz):
        return (z + dz + NZ) % NZ

    def yi(dy):
        return (y + dy + NY) % NY

    def xi(dx):
        return (x + dx + NX) % NX

    copies = []

    def send(src, dst, target_device):
        number = len(copies)
        copy = pltpu.make_async_remote_copy(
            src_ref=src, dst_ref=dst, send_sem=send_sems.at[number], recv_sem=recv_sems.at[number],
            device_id=target_device, device_id_type=pl.DeviceIdType.MESH,
        )
        copy.start()
        copies.append(copy)
        return copy

    locals_ = []

    def local(src, dst):
        copy = pltpu.make_async_copy(src, dst, local_sems.at[len(locals_)])
        copy.start()
        locals_.append(copy)
        return copy

    own_rows = pl.ds(pl.multiple_of(xh * 64, 64), 64)
    l_proj = []
    for r in range(2):
        cols = pl.ds(pl.multiple_of(core * HALF + r * QUARTER, QUARTER), QUARTER)
        l_proj.append(local(proj.at[:, cols], pbuf.at[r, z, y, own_rows]))
    l_emb = local(emb, ebuf.at[pl.ds(pl.multiple_of(core * 128, 128), 128)])
    j_rows = pl.ds(pl.multiple_of(xh * CENTS, CENTS), CENTS)
    other_rows = pl.ds(pl.multiple_of((1 - xh) * CENTS, CENTS), CENTS)
    my_docs = pl.ds(pl.multiple_of(xh * 512, 512), 512)
    l_cent = local(cent.at[j_rows], cbuf)
    l_tgt = local(target.at[:, j_rows], tbuf.at[my_docs])

    ring = [(dx, dc) for dx in range(NX) for dc in range(2) if (dx, dc) != (0, 0)]
    peers = [device(dx=dx, dc=dc) for dx, dc in ring]
    peers += [device(dz=d) for d in range(1, NZ)] + [device(dy=d) for d in range(1, NY)]
    barrier = pltpu.get_barrier_semaphore()
    for peer in peers:
        pl.semaphore_signal(barrier, inc=1, device_id=peer, device_id_type=pl.DeviceIdType.MESH)
    pl.semaphore_wait(barrier, len(peers))

    other_half = pl.ds(pl.multiple_of((1 - xh) * 64, 64), 64)

    class Gather:
        def __init__(self, r):
            self.buf = pbuf.at[r]
            self.bz, self.az, self.ay, self.by = {}, {}, {}, {}

        def move(self, part, at_z, at_y, **hop):
            where = self.buf.at[zi(at_z), yi(at_y), own_rows if part == "a" else other_half]
            return send(where, where, device(**hop))

        def move_half(self, half, at_z, **hop):
            start = pl.multiple_of(xh * 64 + half * 32, 32)
            where = self.buf.at[zi(at_z), y, pl.ds(start, 32)]
            return send(where, where, device(**hop))

        def b_own(self, q):
            for sign in (1, -1):
                self.bz[q, sign, 1] = self.move("b", 0, q, dz=sign)

        def b_y(self, hop):
            self.by[hop].wait_recv()
            self.b_own(2 if hop == 2 else -hop)

        def b_step(self, step, q):
            for sign in (1, -1):
                if (q, sign, step) in self.bz:
                    self.bz[q, sign, step].wait_recv()
                    if step < 3 or (step == 3 and (sign == 1) == (q in (0, 2))):
                        self.bz[q, sign, step + 1] = self.move("b", -sign * step, q, dz=sign)

        def a_y_sends(self, dz):
            for sign in (1, -1):
                self.ay[dz, sign] = self.move("a", dz, 0, dy=sign)

        def a_y_forward(self, dz):
            sign = 1 if dz % 2 == 0 else -1
            self.ay[dz, sign].wait_recv()
            self.ay[dz, 2] = self.move("a", dz, -sign, dy=sign)

        def a_step(self, step):
            for sign in (1, -1):
                self.az[sign, step].wait_recv()
                if step < 3:
                    self.az[sign, step + 1] = self.move("a", -sign * step, 0, dz=sign)
                elif step == 3:
                    self.az[sign, 4] = self.move_half(0 if sign == 1 else 1, -sign * step, dz=sign)
            self.a_y_sends(step)
            if step < 4:
                self.a_y_sends(-step)

        def group(self, g):
            if g == 0:
                where = self.buf.at[z, y, own_rows]
                self.x_swap = send(where, where, to_device(3 - x))
                for sign in (1, -1):
                    self.az[sign, 1] = self.move("a", 0, 0, dz=sign)
                self.a_y_sends(0)
            elif g == 1:
                self.x_swap.wait_recv()
                self.b_own(0)
                for hop in (1, -1, 2):
                    self.by[hop] = self.move("b", 0, 0, dy=hop)
            elif g in (2, 4, 7, 10):
                self.a_step({2: 1, 4: 2, 7: 3, 10: 4}[g])
            elif g == 3:
                self.a_y_forward(0)
            elif g == 5:
                for hop in (1, -1, 2):
                    self.b_y(hop)
                self.b_step(1, 0)
            elif g in (6, 9, 12):
                step = g // 3 - 1
                self.a_y_forward(step)
                self.a_y_forward(-step)
                if step == 3:
                    self.a_y_forward(4)
            elif g in (8, 11, 13):
                step = {8: 1, 11: 2, 13: 3}[g]
                for q in (-1, 1, 2):
                    self.b_step(step, q)
                if step < 3:
                    self.b_step(step + 1, 0)
            else:
                for q in (0, -1, 1, 2):
                    self.b_step(4, q)
                for dz in (0, 1, -1, 2, -2, 3, -3, 4):
                    self.ay[dz, -1 if dz % 2 == 0 else 1].wait_recv()
                    self.ay[dz, 2].wait_recv()

    me8 = x * 2 + core

    def put_stat(stat, block, partial):
        cols = pl.ds(pl.multiple_of((block % 4) * 128, 128), 128)
        early[me8, block // 4, stat:stat + 1, cols] = jnp.sum(partial.T, axis=0, keepdims=True)

    def target_stats(block):
        rows = pl.ds(pl.multiple_of(block * 128, 128), 128)
        wp = jnp.zeros((128, 128), f32)
        lp = jnp.zeros((128, 128), f32)
        for lane in range(8):
            t = tbuf[rows, lane * 128:(lane + 1) * 128].astype(f32)
            wp = wp + t
            lp = lp + t * jnp.log(t)
        put_stat(0, block, wp)
        put_stat(1, block, lp)

    def centroid_block(j):
        cols = pl.ds(pl.multiple_of(j * 128, 128), 128)
        c = cbuf[cols, :].astype(f32).T
        ct[:, cols] = c.astype(bf16)
        cn_ref[0:1, cols] = jnp.sum(c * c, axis=0, keepdims=True)

    rounds = [Gather(0), Gather(1)]
    fx, fc = {}, {}

    def chip_rows(dx):
        return pl.ds(pl.multiple_of(xi(dx) * CHIP_DOCS, CHIP_DOCS), CHIP_DOCS)

    def feat_send(r, at_x, **hop):
        where = feat.at[2 * core + r, chip_rows(at_x)]
        return send(where, where, device(**hop))

    def finish_round(r):
        rounds[r].group(14)
        if r == 0:
            e_copy.wait_recv()
        own = jnp.dot(ebuf[...], pbuf[r].reshape(DIN, QUARTER), preferred_element_type=f32)
        feat[2 * core + r, chip_rows(0), :] = own.astype(bf16)
        fx[r, 1] = feat_send(r, 0, dx=1)
        fx[r, 3] = feat_send(r, 0, dx=-1)
        fc[r, 0] = feat_send(r, 0, dc=1)
        fx[r, 2] = feat_send(r, 0, dx=2)

    l_proj[0].wait()
    rounds[0].group(0)
    l_emb.wait()
    mine = ebuf.at[pl.ds(pl.multiple_of(core * 128, 128), 128)]
    e_copy = send(mine, mine, device(dc=1))
    early[me8] = jnp.zeros((2, 4, 512), f32)
    late[me8] = jnp.zeros((8, 128), f32)
    l_proj[1].wait()
    rounds[1].group(0)
    rounds[0].group(1)
    rounds[1].group(1)
    t_copy = send(target.at[:, other_rows], tbuf.at[my_docs], device(dx=2))
    l_cent.wait()
    l_tgt.wait()
    rounds[0].group(2)
    rounds[0].group(3)
    rounds[0].group(4)
    rounds[0].group(5)
    rounds[0].group(6)
    rounds[1].group(2)
    centroid_block(0)
    rounds[0].group(7)
    rounds[1].group(3)
    rounds[0].group(8)
    centroid_block(1)
    rounds[1].group(4)
    rounds[0].group(9)
    rounds[1].group(5)
    centroid_block(2)
    rounds[0].group(10)
    rounds[1].group(6)
    rounds[0].group(11)
    centroid_block(3)
    rounds[1].group(7)
    rounds[0].group(12)
    rounds[1].group(8)
    centroid_block(4)
    rounds[0].group(13)
    rounds[1].group(9)
    rounds[1].group(10)
    centroid_block(5)
    rounds[1].group(11)
    rounds[1].group(12)
    finish_round(0)
    rounds[1].group(13)
    centroid_block(6)
    centroid_block(7)
    target_stats(xh * 4 + 0)
    target_stats(xh * 4 + 1)
    target_stats(xh * 4 + 2)
    target_stats(xh * 4 + 3)
    gathered = len(copies)
    finish_round(1)

    def inner(dx):
        fc[0, dx].wait_recv()
        fc[1, dx].wait_recv()
        rows = chip_rows(dx)
        parts = [feat[i, rows, :] for i in range(4)]
        f = jnp.concatenate(parts, axis=1)
        g = jnp.dot(f, ct[...], preferred_element_type=f32)
        sq = jnp.zeros((CHIP_DOCS, QUARTER), f32)
        for part in parts:
            sq = sq + part.astype(f32) * part.astype(f32)
        zn = 1.0 + jnp.sum(sq, axis=1, keepdims=True)
        kp = jnp.zeros((CHIP_DOCS, 128), f32)
        cp = jnp.zeros((CHIP_DOCS, 128), f32)
        for lane in range(8):
            cols = slice(lane * 128, (lane + 1) * 128)
            u = (zn + cn_ref[0:1, cols]) - 2.0 * g[:, cols]
            r = pl.reciprocal(u, approx=True)
            k = r * (2.0 - u * r)
            kbuf[rows, cols] = k
            kp = kp + k
            cp = cp + tbuf[rows, cols].astype(f32) * jnp.log(u)
        for h in range(2):
            half = slice(h * 128, (h + 1) * 128)
            if dx == 2:
                late[me8, h:h + 1, :] = jnp.sum(kp[half].T, axis=0, keepdims=True)
                late[me8, 2 + h:3 + h, :] = jnp.sum(cp[half].T, axis=0, keepdims=True)
            else:
                put_stat(2, xi(dx) * 2 + h, kp[half])
                put_stat(3, xi(dx) * 2 + h, cp[half])

    def transpose_features(dx):
        rows = chip_rows(dx)
        for i in range(4):
            ft[i * QUARTER:(i + 1) * QUARTER, rows] = feat[i, rows, :].astype(f32).T.astype(bf16)

    t_copy.wait_recv()

    @pl.loop(0, 4)
    def _(i):
        target_stats((1 - xh) * 4 + i)

    def pass_on(r, dx):
        fx[r, dx].wait_recv()
        fc[r, NX - dx] = feat_send(r, NX - dx, dc=1)

    for dx in (1, 3, 2):
        pass_on(0, dx)
    inner(0)
    transpose_features(0)
    for copy in copies[:gathered]:
        copy.wait_send()
    pass_on(1, 1)
    pass_on(1, 3)
    inner(1)
    pass_on(1, 2)
    inner(3)
    st = [send(early.at[me8], early.at[me8], device(dx=dx, dc=dc)) for dx, dc in ring]
    inner(2)
    st += [send(late.at[me8], late.at[me8], device(dx=dx, dc=dc)) for dx, dc in ring]
    for dx in (1, 3, 2):
        transpose_features(dx)
    for copy in st:
        copy.wait_recv()

    def lanes(parts):
        return jnp.concatenate(parts, axis=1)

    def totals(stat):
        tot = jnp.zeros((1, RING_DOCS), f32)
        for i in range(8):
            tot = tot + lanes([early[i, 0, stat:stat + 1, :], early[i, 1, stat:stat + 1, :]])
        if stat < 2:
            return tot
        for c in range(2):
            tot = tot + lanes([
                late[2 * ((b // 2 + 2) % 4) + c, (stat - 2) * 2 + b % 2:(stat - 2) * 2 + b % 2 + 1, :]
                for b in range(8)
            ])
        return tot

    wsum, ksum = totals(0), totals(2)
    ra, rb = SCALE / wsum, SCALE / ksum
    for block in range(8):
        rows = slice(block * 128, (block + 1) * 128)
        ab[0, rows, :] = jnp.broadcast_to(ra[:, rows], (128, 128)).T
        ab[1, rows, :] = jnp.broadcast_to(rb[:, rows], (128, 128)).T

    colg_ref[...] = jnp.zeros((8, CENTS), f32)

    @pl.loop(0, 8)
    def _(block):
        rows = pl.ds(pl.multiple_of(block * 128, 128), 128)
        a, b = ab[0, rows, :], ab[1, rows, :]
        rp = jnp.zeros((128, 128), f32)
        for lane in range(8):
            cols = slice(lane * 128, (lane + 1) * 128)
            k = kbuf[rows, cols]
            cf = (k * (tbuf[rows, cols].astype(f32) * a - k * b)).astype(bf16)
            cbf[rows, cols] = cf
            cf = cf.astype(f32)
            rp = rp + cf
            colg_ref[:, cols] += jnp.sum(cf.reshape(16, 8, 128), axis=0)
        rowg_ref[rows, :] = jnp.broadcast_to(jnp.sum(rp, axis=1, keepdims=True), (128, 128))

    colg = jnp.sum(colg_ref[...], axis=0, keepdims=True)
    fwd, one, comb, zs, zfirst, yb = {}, {}, {}, {}, {}, {}

    def push_pair(first):
        rows = [pl.ds(pl.multiple_of(zi(ORDER[i]) * 128, 128), 128) for i in (first, first + 1)]
        lhs = jnp.concatenate([ft[r, :] for r in rows], axis=0)
        prod = jnp.dot(lhs, cbf[...], preferred_element_type=f32)
        for k, i in enumerate((first, first + 1)):
            part = prod[k * 128:(k + 1) * 128]
            part = -2.0 * (part - colg * ct[rows[k], :].astype(f32))
            part = part.astype(bf16)
            rs[i] = part[:, :Y_FIRST].reshape(4, 32, Y_FIRST)
            zb[i] = part[:, Y_FIRST:]
            sign = 1 if i % 2 == 0 else -1
            fwd[i] = send(rs.at[i, yi(2)], rfwd.at[i], device(dy=sign))
            one[i] = send(rs.at[i, yi(-sign)], rone.at[i], device(dy=-sign))
            if ORDER[i] != 0:
                zfirst[i] = send(zb.at[i], zbr.at[i], device(dz=ORDER[i]))

    def combine(i):
        sign = 1 if i % 2 == 0 else -1
        fwd[i].wait_recv()
        csend[i] = (rs[i, yi(sign)].astype(f32) + rfwd[i].astype(f32)).astype(bf16)
        comb[i] = send(csend.at[i], rcomb.at[i], device(dy=sign))

    def y_total(i):
        one[i].wait_recv()
        comb[i].wait_recv()
        total = rs[i, y].astype(f32) + rone[i].astype(f32) + rcomb[i].astype(f32)
        if ORDER[i] == 0:
            ysum[:, :Y_FIRST] = total
        else:
            zsend[i] = total.astype(bf16)
            zs[i] = send(zsend.at[i], zrecv.at[i], device(dz=ORDER[i]))

    def z_first_total():
        total = zb[7].astype(f32)
        for i in range(7):
            zfirst[i].wait_recv()
            total = total + zbr[i].astype(f32)
        ybs[...] = total.astype(bf16).reshape(4, 32, Z_FIRST)
        for d in range(1, NY):
            yb[d] = send(ybs.at[yi(d)], ybr.at[d - 1], device(dy=d))

    def pull_block(dx):
        rows = chip_rows(dx)
        pull = jnp.dot(cbf[rows, :], cbuf[...], preferred_element_type=f32)
        rg = rowg_ref[rows, :]
        blocks = []
        for h in range(4):
            f = feat[h, rows, :].astype(f32)
            rgw = jnp.concatenate([rg] * 2, axis=1)
            blocks.append(2.0 * (rgw * f - pull[:, h * QUARTER:(h + 1) * QUARTER]))
        part = jnp.concatenate(blocks, axis=1)
        psend[dx % NX, 0] = part[0:128].astype(bf16)
        psend[dx % NX, 1] = part[128:256].astype(bf16)
        return send(psend.at[dx % NX, 1 - core], precv.at[dx % NX], device(dc=1))

    pulls, gs = {}, {}

    def pull_sum(dx):
        pulls[dx].wait_recv()
        both = psend[dx, core].astype(f32) + precv[dx].astype(f32)
        if dx == 0:
            pown[...] = both
        else:
            gsend[dx - 1] = both.astype(bf16)
            gs[dx] = send(gsend.at[dx - 1], gx.at[dx - 1], device(dx=dx))

    push_pair(0)
    push_pair(2)
    tlog, clog = totals(1), totals(3)
    row_loss = (tlog + clog) / wsum - jnp.log(wsum) + jnp.log(ksum)
    ly[y] = jnp.broadcast_to(jnp.sum(row_loss, axis=1, keepdims=True), (8, 128))
    lsy = [send(ly.at[y], ly.at[y], device(dy=d)) for d in range(1, NY)]
    pulls[2] = pull_block(2)
    combine(0)
    combine(1)
    push_pair(4)
    pulls[1] = pull_block(1)
    pull_sum(2)
    combine(2)
    combine(3)
    push_pair(6)
    pulls[3] = pull_block(3)
    pull_sum(1)
    z_first_total()
    y_total(0)
    y_total(1)
    pulls[0] = pull_block(0)
    pull_sum(3)
    combine(4)
    combine(5)
    for copy in lsy:
        copy.wait_recv()
    lz[z] = (ly[0] + ly[1]) + (ly[2] + ly[3])
    lsz = [send(lz.at[z], lz.at[z], device(dz=d)) for d in range(1, NZ)]
    y_total(2)
    y_total(3)
    pull_sum(0)
    combine(6)
    combine(7)
    y_total(4)
    y_total(5)
    y_total(6)
    y_total(7)
    for dx in (1, 3, 2):
        gs[dx].wait_recv()
    gp_ref[...] = pown[...] + gx[0].astype(f32) + gx[1].astype(f32) + gx[2].astype(f32)
    for copy in lsz:
        copy.wait_recv()
    total = lz[0]
    for i in range(1, NZ):
        total = total + lz[i]
    loss_ref[...] = total * (1.0 / DOCS)
    for d in range(1, NY):
        yb[d].wait_recv()
    for i in range(7):
        zs[i].wait_recv()
    def final(h):
        rows = pl.ds(pl.multiple_of(h * 16, 16), 16)
        a, b = ysum[rows, :Y_FIRST], ybs[y, rows, :].astype(f32)
        for i in range(7):
            a = a + zrecv[i, rows, :].astype(f32)
        for i in range(3):
            b = b + ybr[i, rows, :].astype(f32)
        return jnp.concatenate([a, b], axis=1)

    xsend[...] = final(1 - xh).astype(bf16)
    last = send(xsend, xrecv, device(dx=2))
    gc_ref[:, j_rows] = final(xh)
    last.wait_recv()
    gc_ref[:, other_rows] = xrecv[...].astype(f32)
    for copy in copies[gathered:]:
        copy.wait_send()


def hand_over(gp, gc, loss, gp_out, gc_out, loss_out):
    gp_out[...] = gp[...]
    gc_out[...] = gc[...]
    loss_out[0, 0] = loss[0, 0]


def per_device(embeddings, projection, centroids, target):
    vmem = pltpu.VMEM
    outs = pl.pallas_call(
        body,
        name="cluster_head",
        out_shape=(
            jax.ShapeDtypeStruct((DOCS_DEV, DZ), f32),
            jax.ShapeDtypeStruct((16, 2 * CENTS), f32),
            jax.ShapeDtypeStruct((8, 128), f32),
        ),
        in_specs=[pl.BlockSpec(memory_space=pl.ANY)] * 4,
        out_specs=(pl.BlockSpec(memory_space=vmem),) * 3,
        scratch_shapes=[
            vmem((2, NZ, NY, 128, QUARTER), bf16),
            vmem((CHIP_DOCS, DIN), bf16),
            vmem((CENTS, DZ), bf16),
            vmem((DZ, CENTS), bf16),
            vmem((RING_DOCS, CENTS), bf16),
            vmem((4, RING_DOCS, QUARTER), bf16),
            vmem((DZ, RING_DOCS), bf16),
            vmem((RING_DOCS, CENTS), f32),
            vmem((RING_DOCS, CENTS), bf16),
            vmem((8, 2, 4, 512), f32),
            vmem((8, 8, 128), f32),
            vmem((2, RING_DOCS, 128), f32),
            vmem((RING_DOCS, 128), f32),
            vmem((8, CENTS), f32),
            vmem((8, CENTS), f32),
            vmem((8, 4, 32, Y_FIRST), bf16),
            vmem((8, 32, Y_FIRST), bf16),
            vmem((8, 32, Y_FIRST), bf16),
            vmem((8, 32, Y_FIRST), bf16),
            vmem((8, 32, Y_FIRST), bf16),
            vmem((7, 32, Y_FIRST), bf16),
            vmem((7, 32, Y_FIRST), bf16),
            vmem((8, 128, Z_FIRST), bf16),
            vmem((7, 128, Z_FIRST), bf16),
            vmem((4, 32, Z_FIRST), bf16),
            vmem((3, 32, Z_FIRST), bf16),
            vmem((32, CENTS), f32),
            vmem((16, CENTS), bf16),
            vmem((16, CENTS), bf16),
            vmem((4, 2, 128, DZ), bf16),
            vmem((128, DZ), f32),
            vmem((4, 128, DZ), bf16),
            vmem((3, 128, DZ), bf16),
            vmem((3, 128, DZ), bf16),
            vmem((NY, 8, 128), f32),
            vmem((NZ, 8, 128), f32),
            pltpu.SemaphoreType.DMA((N_SEM,)),
            pltpu.SemaphoreType.DMA((N_SEM,)),
            pltpu.SemaphoreType.DMA((5,)),
        ],
        compiler_params=pltpu.CompilerParams(
            collective_id=0, has_side_effects=True, vmem_limit_bytes=60 * 2**20
        ),
        cost_estimate=pl.CostEstimate(flops=7_500_000_000, bytes_accessed=9_000_000, transcendentals=3_000_000),
    )(embeddings, projection, centroids, target)
    gp, gct, loss = pl.pallas_call(
        hand_over,
        name="hand_over",
        out_shape=(
            jax.ShapeDtypeStruct((DOCS_DEV, DZ), f32),
            jax.ShapeDtypeStruct((16, 2 * CENTS), f32),
            jax.ShapeDtypeStruct((1, 1), f32),
        ),
        in_specs=[pl.BlockSpec(memory_space=vmem)] * 3,
        out_specs=(pl.BlockSpec(memory_space=vmem),) * 2 + (pl.BlockSpec(memory_space=pltpu.SMEM),),
    )(*outs)
    return gp, gct.T, loss.reshape(())


def solution(mesh):
    placed = (P(("wide", "narrow"), None), P("wide", None), P("narrow", None), P("wide", "narrow"))
    return jax.shard_map(
        per_device,
        mesh=mesh,
        in_specs=placed,
        out_specs=(P(("wide", "narrow"), None), P("narrow", "wide"), P()),
        check_vma=False,
    )
```
